32 devices in a mesh: groups: 2 (over x), rows: 8 (over z, y), cols: 2 (over core).
Axes of the slice: x: 2, y: 2, z: 4, core: 2. Of those that a mesh axis runs over, the one named last changes fastest.
Arguments:
- weather: bfloat16 [128, 512, 256], P(('groups', 'rows'), 'cols'), parts along dimension 0, may hold values from -6 to 6
- pre_scale: float32 [256], replicated, may hold values from 0.5 to 1.5
- pre_shift: float32 [256], replicated, may hold values from -2 to 2
- w_expand: bfloat16 [256, 1024], replicated, may hold values from -0.375 to 0.375
- ex_scale: float32 [1024], replicated, may hold values from 0.5 to 1.5
- ex_shift: float32 [1024], replicated, may hold values from -2 to 2
- dw_kernel: float32 [3, 3, 1024], replicated, may hold values from -2 to 2
- dw_scale: float32 [1024], replicated, may hold values from 0.5 to 1.5
- dw_shift: float32 [1024], replicated, may hold values from -2 to 2
- w_project: bfloat16 [1024, 256], replicated, may hold values from -0.1875 to 0.1875
- win_gain: float32 [256], replicated, may hold values from 0.5 to 1.5
- win_qkv: bfloat16 [256, 768], replicated, may hold values from -0.375 to 0.375
- win_out: bfloat16 [256, 256], replicated, may hold values from -0.375 to 0.375
- win_table: float32 [8, 225], replicated, may hold values from -2 to 320, as said below
- winff_gain: float32 [256], replicated, may hold values from 0.5 to 1.5
- winff_up: bfloat16 [256, 1024], replicated, may hold values from -0.375 to 0.375
- winff_down: bfloat16 [1024, 256], replicated, may hold values from -0.1875 to 0.1875
- grid_gain: float32 [256], replicated, may hold values from 0.5 to 1.5
- grid_qkv: bfloat16 [256, 768], replicated, may hold values from -0.375 to 0.375
- grid_out: bfloat16 [256, 256], replicated, may hold values from -0.375 to 0.375
- grid_table: float32 [8, 225], replicated, may hold values from -2 to 320, as said below
- gridff_gain: float32 [256], replicated, may hold values from 0.5 to 1.5
- gridff_up: bfloat16 [256, 1024], replicated, may hold values from -0.375 to 0.375
- gridff_down: bfloat16 [1024, 256], replicated, may hold values from -0.1875 to 0.1875
Outputs:
- block_out: bfloat16 [128, 512, 256], P(('groups', 'rows'), 'cols'), parts along dimension 0
The draws below stay inside these ranges and needn't reach their ends.
There are 2 independent parts, one for each index of `groups`. The reference program is written for one: setup_inputs(seed, part) draws one part's arguments, and reference() takes and returns one part's arrays. A program takes and returns all parts, laid end to end along the dimension named above; an argument that names none is the same for every part. Nothing has to cross between parts.
Inputs may be any that keep to these rules, and one draw needn't show every extreme that they name: `win_table`: bias of window attention over relative offsets. In some draws each head's entries at the offsets (7, 7) and (7, 6), columns 224 and 223, reach up to 320 and differ by 1 to 3; all other entries lie within -2 to 2. `grid_table`: bias of grid attention over relative offsets. In some draws each head's entries at the offsets (7, 7) and (7, 6), columns 224 and 223, reach up to 320 and differ by 1 to 3; all other entries lie within -2 to 2.
All inputs are finite; a program needn't handle non-finite values.
Results may differ from the reference program's by a relative error of at most 0.014.
Values may be sent and summed in bfloat16 or wider, within the bound.
A program may use at most 64 MiB of HBM per device.

```python
import jax
import jax.numpy as jnp
from jax import lax

C = 256
HEADS = 8
WIN = 8
EXPAND = 1024
REL = 225
H = 64
W = 512
N_ROWS = 8


def base_table(key):
    return jnp.clip(jax.random.normal(key, (HEADS, REL), jnp.float32) * 0.5, -2.0, 2.0)


def draw_win_table(key, part):
    key = jax.random.fold_in(key, 11)
    table = base_table(key)
    return table


def draw_grid_table(key, part):
    key = jax.random.fold_in(key, 23)
    table = base_table(key)
    return table


def steps_of(stream_key, shape, pieces, low, high):
    def one(axis_at, blocks):
        steps = jax.random.uniform(jax.random.fold_in(jax.random.fold_in(stream_key, 6), axis_at), (blocks,), jnp.float32, low / len(pieces), high / len(pieces))
        return jnp.repeat(jnp.exp(steps), shape[axis_at] // blocks).reshape((-1,) + (1,) * (len(shape) - axis_at - 1))

    level = one(*pieces[0])
    for cut in pieces[1:]:
        level = level * one(*cut)
    return level


def gaussian(key, extent, scale, bound, cuts=(), held_as=jnp.bfloat16):
    drawn = jax.random.normal(key, extent, jnp.float32) * scale
    if len(cuts) > 0:
        drawn = steps_of(key, extent, cuts, -0.22, 0.18) * drawn
    return jnp.clip(drawn, min=-bound, max=bound).astype(held_as)


def setup_inputs(seed: int = 0, part: int = 0) -> dict:
    streams_of = jax.random.split(jax.random.key(seed), 25)
    own_keys = jax.random.split(jax.random.fold_in(streams_of[24], part), 25)
    weather = gaussian(own_keys[0], (H, W, C), 1.0, 6.0, ((0, 8), (1, 2)))
    pre_scale = jnp.clip(1.0 + 0.1 * jax.random.normal(streams_of[1], (C,), jnp.float32), 0.5, 1.5)
    pre_shift = gaussian(streams_of[2], (C,), 0.5, 2.0, (), jnp.float32)
    w_expand = gaussian(streams_of[3], (C, EXPAND), C ** -0.5, 0.375)
    ex_scale = jnp.clip(1.0 + 0.1 * jax.random.normal(streams_of[4], (EXPAND,), jnp.float32), 0.5, 1.5)
    ex_shift = gaussian(streams_of[5], (EXPAND,), 0.5, 2.0, (), jnp.float32)
    dw_kernel = gaussian(streams_of[6], (3, 3, EXPAND), 9 ** -0.5, 2.0, (), jnp.float32)
    dw_scale = jnp.clip(1.0 + 0.1 * jax.random.normal(streams_of[7], (EXPAND,), jnp.float32), 0.5, 1.5)
    dw_shift = gaussian(streams_of[8], (EXPAND,), 0.5, 2.0, (), jnp.float32)
    w_project = gaussian(streams_of[9], (EXPAND, C), EXPAND ** -0.5, 0.1875)
    win_gain = jnp.clip(1.0 + 0.1 * jax.random.normal(streams_of[10], (C,), jnp.float32), 0.5, 1.5)
    win_qkv = gaussian(streams_of[11], (C, 3 * C), C ** -0.5, 0.375)
    win_out = gaussian(streams_of[12], (C, C), C ** -0.5, 0.375)
    win_table = draw_win_table(jax.random.fold_in(streams_of[24], 71), part)
    winff_gain = jnp.clip(1.0 + 0.1 * jax.random.normal(streams_of[14], (C,), jnp.float32), 0.5, 1.5)
    winff_up = gaussian(streams_of[15], (C, EXPAND), C ** -0.5, 0.375)
    winff_down = gaussian(streams_of[16], (EXPAND, C), EXPAND ** -0.5, 0.1875)
    grid_gain = jnp.clip(1.0 + 0.1 * jax.random.normal(streams_of[17], (C,), jnp.float32), 0.5, 1.5)
    grid_qkv = gaussian(streams_of[18], (C, 3 * C), C ** -0.5, 0.375)
    grid_out = gaussian(streams_of[19], (C, C), C ** -0.5, 0.375)
    grid_table = draw_grid_table(jax.random.fold_in(streams_of[24], 71), part)
    gridff_gain = jnp.clip(1.0 + 0.1 * jax.random.normal(streams_of[21], (C,), jnp.float32), 0.5, 1.5)
    gridff_up = gaussian(streams_of[22], (C, EXPAND), C ** -0.5, 0.375)
    gridff_down = gaussian(streams_of[23], (EXPAND, C), EXPAND ** -0.5, 0.1875)
    return dict(weather=weather, pre_scale=pre_scale, pre_shift=pre_shift, w_expand=w_expand, ex_scale=ex_scale, ex_shift=ex_shift, dw_kernel=dw_kernel, dw_scale=dw_scale, dw_shift=dw_shift, w_project=w_project, win_gain=win_gain, win_qkv=win_qkv, win_out=win_out, win_table=win_table, winff_gain=winff_gain, winff_up=winff_up, winff_down=winff_down, grid_gain=grid_gain, grid_qkv=grid_qkv, grid_out=grid_out, grid_table=grid_table, gridff_gain=gridff_gain, gridff_up=gridff_up, gridff_down=gridff_down)


def rel_bias(table):
    cells = jnp.arange(WIN * WIN)
    prow = cells // WIN
    pcol = cells % WIN
    offset = (prow[:, None] - prow[None, :] + WIN - 1) * (2 * WIN - 1) + (pcol[:, None] - pcol[None, :] + WIN - 1)
    onehot = (offset[:, :, None] == jnp.arange((2 * WIN - 1) * (2 * WIN - 1))[None, None, :]).astype(jnp.float32)
    return jnp.einsum('qkt,ht->hqk', onehot, table, precision=lax.Precision.HIGHEST)

def layer_norm(stream, gain):
    center = stream - lax.optimization_barrier(jnp.mean(stream, axis=-1, keepdims=True))
    spread = lax.optimization_barrier(jnp.mean(center * center, axis=-1, keepdims=True))
    return center * lax.rsqrt(spread + 1e-05) * gain

def attend(stream, gain, w_qkv, w_out, bias):
    groups, length, width = stream.shape
    normed = layer_norm(stream, gain).astype(jnp.bfloat16)
    qkv = jnp.einsum('gtc,cf->gtf', normed.astype(jnp.float32), w_qkv.astype(jnp.float32)).astype(jnp.bfloat16)
    qkv = qkv.reshape(groups, length, 3, HEADS, width // HEADS)
    query = qkv[:, :, 0].astype(jnp.float32)
    keys = qkv[:, :, 1].astype(jnp.float32)
    values = qkv[:, :, 2].astype(jnp.float32)
    scores = jnp.einsum('gqhd,gkhd->ghqk', query, keys) * (width // HEADS) ** (-0.5) + bias[None]
    probs = jax.nn.softmax(scores, axis=-1).astype(jnp.bfloat16)
    mixed = jnp.einsum('ghqk,gkhd->gqhd', probs.astype(jnp.float32), values).astype(jnp.bfloat16)
    mixed = mixed.reshape(groups, length, width)
    return stream + jnp.einsum('gtc,cf->gtf', mixed.astype(jnp.float32), w_out.astype(jnp.float32))

def feed(stream, gain, w_up, w_down):
    normed = layer_norm(stream, gain).astype(jnp.bfloat16)
    hidden = jax.nn.gelu(jnp.einsum('gtc,cf->gtf', normed.astype(jnp.float32), w_up.astype(jnp.float32))).astype(jnp.bfloat16)
    return stream + jnp.einsum('gtf,fc->gtc', hidden.astype(jnp.float32), w_down.astype(jnp.float32))

def reference(weather, pre_scale, pre_shift, w_expand, ex_scale, ex_shift, dw_kernel, dw_scale, dw_shift, w_project, win_gain, win_qkv, win_out, win_table, winff_gain, winff_up, winff_down, grid_gain, grid_qkv, grid_out, grid_table, gridff_gain, gridff_up, gridff_down):
    inputs = weather.astype(jnp.float32)
    normed_in = (inputs * pre_scale + pre_shift).astype(jnp.bfloat16)
    expanded = jnp.dot(normed_in.reshape(H * W, C), w_expand, preferred_element_type=jnp.float32)
    expanded = jax.nn.gelu(expanded * ex_scale + ex_shift).astype(jnp.bfloat16).reshape(H, W, EXPAND)
    padded = jnp.pad(expanded, ((1, 1), (1, 1), (0, 0)))
    total = jnp.zeros((H, W, EXPAND), jnp.float32)
    for arow in range(3):
        for bcol in range(3):
            total = total + padded[arow:arow + H, bcol:bcol + W].astype(jnp.float32) * dw_kernel[arow, bcol]
    depth = jax.nn.gelu(total * dw_scale + dw_shift).astype(jnp.bfloat16)
    section_one = inputs + jnp.dot(depth.reshape(H * W, EXPAND), w_project, preferred_element_type=jnp.float32).reshape(H, W, C)
    section_one = section_one.astype(jnp.bfloat16)
    win_bias = rel_bias(win_table)
    grid_bias = rel_bias(grid_table)

    def window_block(block):
        stream = attend(block.astype(jnp.float32), win_gain, win_qkv, win_out, win_bias)
        return feed(stream, winff_gain, winff_up, winff_down).astype(jnp.bfloat16)

    def grid_block(block):
        stream = attend(block.astype(jnp.float32), grid_gain, grid_qkv, grid_out, grid_bias)
        return feed(stream, gridff_gain, gridff_up, gridff_down).astype(jnp.bfloat16)
    windows = section_one.reshape(H // WIN, WIN, W // WIN, WIN, C).transpose(0, 2, 1, 3, 4).reshape(N_ROWS, -1, WIN * WIN, C)
    section_three = lax.map(window_block, windows)
    section_three = section_three.reshape(H // WIN, W // WIN, WIN, WIN, C).transpose(0, 2, 1, 3, 4).reshape(H, W, C)
    gridded = section_three.reshape(WIN, H // WIN, WIN, W // WIN, C).transpose(1, 3, 0, 2, 4).reshape(N_ROWS, -1, WIN * WIN, C)
    block_out = lax.map(grid_block, gridded)
    block_out = block_out.reshape(H // WIN, W // WIN, WIN, WIN, C).transpose(2, 0, 3, 1, 4).reshape(H, W, C)
    return block_out
```

```python
import functools
import math

import jax
import jax.numpy as jnp
from jax import lax
from jax.experimental import pallas as pl
from jax.experimental.pallas import tpu as pltpu
from jax.sharding import PartitionSpec as P

WIN = 8
BF = jnp.bfloat16
F32 = jnp.float32
LOG2E = math.log2(math.e)
NT = (((1,), (1,)), ((), ()))
TN = (((0,), (0,)), ((), ()))


def extended(cells, sides, width):
    for axis, dim in sides:
        count = lax.axis_size(axis)
        ends = count - 1
        head = lax.slice_in_dim(cells, 0, width, axis=dim)
        tail = lax.slice_in_dim(cells, cells.shape[dim] - width, cells.shape[dim], axis=dim)
        cells = jnp.concatenate(
            [
                lax.ppermute(tail, axis, [(i, (i + 1) % count) for i in range(ends)]),
                cells,
                lax.ppermute(head, axis, [((i + 1) % count, i) for i in range(ends)]),
            ],
            axis=dim,
        )
    return cells


def bias_keys_first(table):
    heads = table.shape[0]
    grid = (table * LOG2E).reshape(heads, 2 * WIN - 1, 2 * WIN - 1)
    rows = jnp.stack([grid[:, WIN - 1 - k : 2 * WIN - 1 - k, :] for k in range(WIN)])
    both = jnp.stack(
        [rows[..., WIN - 1 - k : 2 * WIN - 1 - k] for k in range(WIN)], axis=1
    )
    return both.reshape(WIN * WIN, heads * WIN * WIN)


def gelu(x):
    c0 = math.sqrt(2.0 / math.pi)
    inner = x * (c0 + (c0 * 0.044715) * (x * x))
    half = 0.5 * x
    return half + half * jnp.tanh(inner)


def norm(x, gain):
    center = x - jnp.mean(x, axis=-1, keepdims=True)
    spread = jnp.mean(center * center, axis=-1, keepdims=True)
    return (center * lax.rsqrt(spread + 1e-05) * gain).astype(BF)


def dot(a, b):
    return jnp.dot(a, b, preferred_element_type=F32)


def attend(x, gain, w_qk, w_vt, w_out, bias):
    width = x.shape[1]
    cells = WIN * WIN
    groups = x.shape[0] // cells
    heads = bias.shape[1] // cells
    dim = width // heads
    scale = dim ** (-0.5) * LOG2E
    n = norm(x, gain)
    qk = dot(n, w_qk).astype(BF)
    vt = lax.dot_general(w_vt, n, NT, preferred_element_type=F32).astype(BF)
    lane_head = lax.broadcasted_iota(jnp.int32, (cells, width), 1) // dim
    probs = []
    for g in range(groups):
        q = qk[g * cells : (g + 1) * cells, :width]
        k = qk[g * cells : (g + 1) * cells, width:]
        spread = jnp.concatenate(
            [jnp.where(lane_head == h, q, jnp.zeros_like(q)) for h in range(heads)], axis=0
        )
        s = lax.dot_general(k, spread, NT, preferred_element_type=F32) * scale + bias
        e = jnp.exp2(s - jnp.max(s, axis=0, keepdims=True))
        e = e * (1.0 / jnp.sum(e, axis=0, keepdims=True))
        probs.append(e.astype(BF))
    low = lax.broadcasted_iota(jnp.int32, (dim, 2 * cells), 1) < cells
    zeros = jnp.zeros((cells, 2 * cells), BF)
    mixed = []
    for g in range(0, groups, 2):
        parts = []
        for t in range(heads // 2):
            at = slice(2 * cells * t, 2 * cells * (t + 1))
            pair = jnp.concatenate(
                [
                    jnp.concatenate([probs[g][:, at], zeros], axis=1),
                    jnp.concatenate([zeros, probs[g + 1][:, at]], axis=1),
                ],
                axis=0,
            )
            v = vt[2 * dim * t : 2 * dim * (t + 1), g * cells : (g + 2) * cells]
            o = dot(v, pair)
            a, b = o[:, : 2 * cells], o[:, 2 * cells :]
            parts.append(jnp.where(low, a[:dim], pltpu.roll(b[:dim], cells, 1)))
            parts.append(jnp.where(low, pltpu.roll(a[dim:], cells, 1), b[dim:]))
        mixed.append(jnp.concatenate(parts, axis=0).astype(BF))
    mixed = jnp.concatenate(mixed, axis=1)
    return x + lax.dot_general(mixed, w_out, TN, preferred_element_type=F32)


def feed(x, gain, up_ref, down_ref, step=256):
    n = norm(x, gain)
    total = x
    for at in range(0, up_ref.shape[1], step):
        hidden = gelu(dot(n, up_ref[:, at : at + step])).astype(BF)
        total = total + dot(hidden, down_ref[at : at + step, :])
    return total


PAD = 8


def first_kernel(
    valid, ext, pre_scale, pre_shift, w_expand, ex_scale, ex_shift, taps, dw_scale, dw_shift,
    w_project, gain, w_qk, w_vt, w_out, bias, ffgain, up, down, out, grown, depth, one,
):
    rows, cols, width = out.shape
    wide = w_expand.shape[1]
    span = ext.shape[1]
    column = lax.broadcasted_iota(jnp.int32, (span, 1), 0)
    edge = jnp.where(column == PAD - 1, valid[2], jnp.where(column == PAD + cols, valid[3], 1.0))

    def expand(r, carry):
        keep = jnp.where(r == 0, valid[0], jnp.where(r == rows + 1, valid[1], 1.0))
        x = (ext[r].astype(F32) * pre_scale[...] + pre_shift[...]).astype(BF)
        for at in range(0, wide, 256):
            s = slice(at, at + 256)
            y = gelu(dot(x, w_expand[:, s]) * ex_scale[:, s] + ex_shift[:, s])
            grown[r, :, s] = (y * (edge * keep)).astype(BF)
        return carry

    lax.fori_loop(0, rows + 2, expand, 0)

    def row(r, carry):
        for lane in range(0, wide, 128):
            ls = slice(lane, lane + 128)
            for c in range(0, cols, 64):
                sums = [None] * 3
                for a in range(3):
                    e = grown[r + a, c : c + 64 + 2 * PAD, ls].astype(F32)
                    for b in range(3):
                        term = e * taps[3 * a + b : 3 * a + b + 1, ls]
                        sums[b] = term if a == 0 else sums[b] + term
                total = (
                    sums[0][PAD - 1 : PAD + 63]
                    + sums[1][PAD : PAD + 64]
                    + sums[2][PAD + 1 : PAD + 65]
                )
                depth[c : c + 64, ls] = gelu(
                    total * dw_scale[:, ls] + dw_shift[:, ls]
                ).astype(BF)
        y = ext[r + 1, PAD : PAD + cols, :].astype(F32) + dot(depth[...], w_project[...])
        one[r] = y.astype(BF).astype(F32)
        return carry

    lax.fori_loop(0, rows, row, 0)

    def window(m, carry):
        pieces = []
        for g in range(4):
            at = pl.multiple_of(m * 32 + g * 8, 8)
            pieces.append(one[:, pl.ds(at, 8), :].reshape(WIN * WIN, width))
        x = jnp.concatenate(pieces, axis=0)
        x = attend(x, gain[...], w_qk[...], w_vt[...], w_out[...], bias[...])
        x = feed(x, ffgain[...], up, down)
        x = x.reshape(4, WIN, WIN, width)
        y = jnp.concatenate([x[g] for g in range(4)], axis=1)
        out[:, pl.ds(pl.multiple_of(m * 32, 32), 32), :] = y.astype(BF)
        return carry

    lax.fori_loop(0, cols // 32, window, 0)


def second_kernel(x_ref, gain, w_qk, w_vt, w_out, bias, ffgain, up, down, out):
    def group(m, carry):
        at = pl.ds(pl.multiple_of(m * 256, 256), 256)
        x = x_ref[at, :].astype(F32)
        x = attend(x, gain[...], w_qk[...], w_vt[...], w_out[...], bias[...])
        out[at, :] = feed(x, ffgain[...], up, down).astype(BF)
        return carry

    lax.fori_loop(0, x_ref.shape[0] // 256, group, 0)


def attention_operands(gain, w_qkv, w_out, table):
    width = w_qkv.shape[0]
    return (
        gain[None],
        w_qkv[:, : 2 * width],
        w_qkv[:, 2 * width :].T,
        w_out,
        bias_keys_first(table),
    )


def local(
    weather, pre_scale, pre_shift, w_expand, ex_scale, ex_shift, dw_kernel, dw_scale, dw_shift,
    w_project, win_gain, win_qkv, win_out, win_table, winff_gain, winff_up, winff_down,
    grid_gain, grid_qkv, grid_out, grid_table, gridff_gain, gridff_up, gridff_down,
):
    tile_rows, tile_cols, width = weather.shape
    wide = w_expand.shape[1]
    side = WIN
    rows_count = lax.axis_size("rows")
    cols_count = lax.axis_size("cols")
    ext = extended(weather, (("rows", 0), ("cols", 1)), 1)
    ext = jnp.pad(ext, ((0, 0), (PAD - 1, PAD - 1), (0, 0)))
    ri, ci = lax.axis_index("rows"), lax.axis_index("cols")
    valid = jnp.stack([ri > 0, ri < rows_count - 1, ci > 0, ci < cols_count - 1]).astype(F32)
    vmem = pl.BlockSpec(memory_space=pltpu.VMEM)
    section_three = pl.pallas_call(
        first_kernel,
        out_shape=jax.ShapeDtypeStruct((tile_rows, tile_cols, width), BF),
        in_specs=[pl.BlockSpec(memory_space=pltpu.SMEM)] + [vmem] * 18,
        out_specs=vmem,
        scratch_shapes=[
            pltpu.VMEM((tile_rows + 2, tile_cols + 2 * PAD, wide), BF),
            pltpu.VMEM((tile_cols, wide), BF),
            pltpu.VMEM((tile_rows, tile_cols, width), F32),
        ],
        compiler_params=pltpu.CompilerParams(vmem_limit_bytes=50 << 20),
        name="mbconv_window",
    )(
        valid, ext, pre_scale[None], pre_shift[None], w_expand, ex_scale[None], ex_shift[None],
        dw_kernel.reshape(9, wide), dw_scale[None], dw_shift[None], w_project,
        *attention_operands(win_gain, win_qkv, win_out, win_table),
        winff_gain[None], winff_up, winff_down,
    )
    quarter = rows_count // side
    places = side // cols_count
    residues = tile_cols // rows_count
    ordered = section_three.reshape(side, places, quarter, cols_count, residues, width).transpose(
        2, 0, 3, 1, 4, 5
    )
    arrived = lax.all_to_all(
        ordered.reshape(rows_count * cols_count, places, residues, width),
        ("rows", "cols"),
        split_axis=0,
        concat_axis=0,
        tiled=True,
    )
    gridded = arrived.reshape(side, quarter, cols_count, places, residues, width).transpose(
        1, 4, 0, 2, 3, 5
    )
    finished = pl.pallas_call(
        second_kernel,
        out_shape=jax.ShapeDtypeStruct((tile_rows * tile_cols, width), BF),
        in_specs=[vmem] * 9,
        out_specs=vmem,
        compiler_params=pltpu.CompilerParams(vmem_limit_bytes=50 << 20),
        name="grid",
    )(
        gridded.reshape(-1, width),
        *attention_operands(grid_gain, grid_qkv, grid_out, grid_table),
        gridff_gain[None], gridff_up, gridff_down,
    )
    finished = finished.reshape(quarter, residues, side, cols_count, places, width).transpose(
        2, 0, 3, 4, 1, 5
    )
    returned = lax.all_to_all(
        finished.reshape(rows_count * cols_count, places, residues, width),
        ("rows", "cols"),
        split_axis=0,
        concat_axis=0,
        tiled=True,
    )
    block_out = returned.reshape(quarter, side, cols_count, places, residues, width).transpose(
        1, 3, 0, 2, 4, 5
    )
    return block_out.reshape(tile_rows, tile_cols, width)


def solution(mesh):
    spread = P(("groups", "rows"), "cols", None)
    return jax.shard_map(
        local,
        mesh=mesh,
        in_specs=(spread,) + (P(),) * 23,
        out_specs=spread,
        check_vma=False,
    )
```

```python
import functools
import math

import jax
import jax.numpy as jnp
from jax import lax
from jax.experimental import pallas as pl
from jax.experimental.pallas import tpu as pltpu
from jax.sharding import PartitionSpec as P

WIN = 8
BF = jnp.bfloat16
F32 = jnp.float32
LOG2E = math.log2(math.e)
NT = (((1,), (1,)), ((), ()))
TN = (((0,), (0,)), ((), ()))


def extended(cells, sides, width):
    for axis, dim in sides:
        count = lax.axis_size(axis)
        ends = count - 1
        head = lax.slice_in_dim(cells, 0, width, axis=dim)
        tail = lax.slice_in_dim(cells, cells.shape[dim] - width, cells.shape[dim], axis=dim)
        cells = jnp.concatenate(
            [
                lax.ppermute(tail, axis, [(i, (i + 1) % count) for i in range(ends)]),
                cells,
                lax.ppermute(head, axis, [((i + 1) % count, i) for i in range(ends)]),
            ],
            axis=dim,
        )
    return cells


def biases_keys_first(tables):
    count, heads, offsets = tables.shape
    cells = WIN * WIN
    pair = jnp.arange(cells * cells)
    k, q = pair // cells, pair % cells
    offset = (q // WIN - k // WIN + WIN - 1) * (2 * WIN - 1) + (q % WIN - k % WIN + WIN - 1)
    onehot = (jnp.arange(offsets)[:, None] == offset[None, :]).astype(F32)
    flat = jnp.dot(
        tables.reshape(count * heads, offsets) * LOG2E, onehot, precision=lax.Precision.HIGHEST
    )
    flat = flat.reshape(count, heads, cells, cells).transpose(0, 2, 1, 3)
    return flat.reshape(count, cells, heads * cells)


def gelu(x):
    c0 = math.sqrt(2.0 / math.pi)
    inner = x * (c0 + (c0 * 0.044715) * (x * x))
    half = 0.5 * x
    return half + half * jnp.tanh(inner)


def norm(x, gain):
    center = x - jnp.mean(x, axis=-1, keepdims=True)
    spread = jnp.mean(center * center, axis=-1, keepdims=True)
    return (center * lax.rsqrt(spread + 1e-05) * gain).astype(BF)


def dot(a, b):
    return jnp.dot(a, b, preferred_element_type=F32)


def attend(x, gain, w_qk, w_vt, w_out, bias):
    width = x.shape[1]
    cells = WIN * WIN
    groups = x.shape[0] // cells
    heads = bias.shape[1] // cells
    dim = width // heads
    scale = dim ** (-0.5) * LOG2E
    n = norm(x, gain)
    qk = dot(n, w_qk).astype(BF)
    vt = lax.dot_general(w_vt, n, NT, preferred_element_type=F32).astype(BF)
    lane_head = lax.broadcasted_iota(jnp.int32, (cells, width), 1) // dim
    probs = []
    for g in range(groups):
        q = qk[g * cells : (g + 1) * cells, :width]
        k = qk[g * cells : (g + 1) * cells, width:]
        spread = jnp.concatenate(
            [jnp.where(lane_head == h, q, jnp.zeros_like(q)) for h in range(heads)], axis=0
        )
        s = lax.dot_general(k, spread, NT, preferred_element_type=F32) * scale + bias
        e = jnp.exp2(s - jnp.max(s, axis=0, keepdims=True))
        e = e * (1.0 / jnp.sum(e, axis=0, keepdims=True))
        probs.append(e.astype(BF))
    low = lax.broadcasted_iota(jnp.int32, (dim, 2 * cells), 1) < cells
    zeros = jnp.zeros((cells, 2 * cells), BF)
    mixed = []
    for g in range(0, groups, 2):
        parts = []
        for t in range(heads // 2):
            at = slice(2 * cells * t, 2 * cells * (t + 1))
            pair = jnp.concatenate(
                [
                    jnp.concatenate([probs[g][:, at], zeros], axis=1),
                    jnp.concatenate([zeros, probs[g + 1][:, at]], axis=1),
                ],
                axis=0,
            )
            v = vt[2 * dim * t : 2 * dim * (t + 1), g * cells : (g + 2) * cells]
            o = dot(v, pair)
            a, b = o[:, : 2 * cells], o[:, 2 * cells :]
            parts.append(jnp.where(low, a[:dim], pltpu.roll(b[:dim], cells, 1)))
            parts.append(jnp.where(low, pltpu.roll(a[dim:], cells, 1), b[dim:]))
        mixed.append(jnp.concatenate(parts, axis=0).astype(BF))
    mixed = jnp.concatenate(mixed, axis=1)
    return x + lax.dot_general(mixed, w_out, TN, preferred_element_type=F32)


def feed(x, gain, up_ref, down_ref, step=256):
    n = norm(x, gain)
    total = x
    for at in range(0, up_ref.shape[1], step):
        hidden = gelu(dot(n, up_ref[:, at : at + step])).astype(BF)
        total = total + dot(hidden, down_ref[at : at + step, :])
    return total


PAD = 8


def block_kernel(
    valid, ext, pre_scale, pre_shift, w_expand, ex_scale, ex_shift, taps, dw_scale, dw_shift,
    w_project, gain, w_qk, w_vt, w_out, bias, ffgain, up, down, gain2, w_qk2, w_vt2, w_out2,
    bias2, ffgain2, up2, down2, out, grown, depth, one, sent, arrived, returned, back, loose,
    sent_sem, arrived_sem, returned_sem, back_sem, *, quarter,
):
    row_at, col_at = lax.axis_index("rows"), lax.axis_index("cols")
    col_count = lax.axis_size("cols")
    peers = WIN * col_count
    me = (row_at // quarter) * col_count + col_at

    def place(peer):
        return {
            "rows": (peer // col_count) * quarter + lax.rem(row_at, quarter),
            "cols": lax.rem(peer, col_count),
        }

    barrier = pltpu.get_barrier_semaphore()

    def greet(k, carry):
        pl.semaphore_signal(
            barrier, 1, device_id=place(lax.rem(me + k, peers)),
            device_id_type=pl.DeviceIdType.MESH,
        )
        return carry

    lax.fori_loop(1, peers, greet, 0)

    def send(m, src, dst, src_sem, dst_sem):
        def one_peer(k, carry):
            peer = lax.rem(me + k, peers)
            pltpu.make_async_remote_copy(
                src_ref=src.at[m, peer],
                dst_ref=dst.at[m, me],
                send_sem=src_sem.at[m],
                recv_sem=dst_sem.at[m],
                device_id=place(peer),
                device_id_type=pl.DeviceIdType.MESH,
            ).start()
            return carry

        lax.fori_loop(1, peers, one_peer, 0)
        dst[m, me] = src[m, me]

    def wait_all(m, ref, sem):
        part = ref.at[m, pl.ds(0, peers - 1)]
        pltpu.make_async_copy(part, part, sem.at[m]).wait()

    rows, cols, width = out.shape
    wide = w_expand.shape[1]
    span = ext.shape[1]
    column = lax.broadcasted_iota(jnp.int32, (span, 1), 0)
    edge = jnp.where(column == PAD - 1, valid[2], jnp.where(column == PAD + cols, valid[3], 1.0))

    def expand(r, carry):
        keep = jnp.where(r == 0, valid[0], jnp.where(r == rows + 1, valid[1], 1.0))
        x = (ext[r].astype(F32) * pre_scale[...] + pre_shift[...]).astype(BF)
        for at in range(0, wide, 256):
            s = slice(at, at + 256)
            y = gelu(dot(x, w_expand[:, s]) * ex_scale[:, s] + ex_shift[:, s])
            grown[r, :, s] = (y * (edge * keep)).astype(BF)
        return carry

    lax.fori_loop(0, rows + 2, expand, 0)

    def row(r, carry):
        for lane in range(0, wide, 128):
            ls = slice(lane, lane + 128)
            for c in range(0, cols, 64):
                sums = [None] * 3
                for a in range(3):
                    e = grown[r + a, c : c + 64 + 2 * PAD, ls].astype(F32)
                    for b in range(3):
                        term = e * taps[3 * a + b : 3 * a + b + 1, ls]
                        sums[b] = term if a == 0 else sums[b] + term
                total = (
                    sums[0][PAD - 1 : PAD + 63]
                    + sums[1][PAD : PAD + 64]
                    + sums[2][PAD + 1 : PAD + 65]
                )
                depth[c : c + 64, ls] = gelu(
                    total * dw_scale[:, ls] + dw_shift[:, ls]
                ).astype(BF)
        y = ext[r + 1, PAD : PAD + cols, :].astype(F32) + dot(depth[...], w_project[...])
        one[r] = y.astype(BF).astype(F32)
        return carry

    lax.fori_loop(0, rows, row, 0)

    pl.semaphore_wait(barrier, peers - 1)
    first_half = lax.rem(lax.broadcasted_iota(jnp.int32, (WIN * WIN, width), 0), WIN) < WIN // 2
    half = WIN // 2
    chunks = cols // 32

    def exchange(a, b):
        firsts = jnp.where(first_half, a, pltpu.roll(b, half, 0))
        seconds = jnp.where(first_half, pltpu.roll(a, WIN * WIN - half, 0), b)
        return firsts, seconds

    def window(m, carry):
        pieces = []
        for g in range(4):
            at = pl.multiple_of(g * (cols // 4) + m * WIN, WIN)
            pieces.append(one[:, pl.ds(at, WIN), :].reshape(WIN * WIN, width))
        x = jnp.concatenate(pieces, axis=0)
        x = attend(x, gain[...], w_qk[...], w_vt[...], w_out[...], bias[...])
        x = feed(x, ffgain[...], up, down)
        x = [x[WIN * WIN * g : WIN * WIN * (g + 1)] for g in range(4)]
        low, high = exchange(x[0], x[1]), exchange(x[2], x[3])
        for c in range(2):
            y = jnp.concatenate(
                [low[c].reshape(WIN, WIN, width), high[c].reshape(WIN, WIN, width)], axis=1
            ).astype(BF)
            for i in range(WIN):
                sent[m, i * 2 + c] = y[i]
        send(m, sent, arrived, sent_sem, arrived_sem)
        return carry

    lax.fori_loop(0, chunks, window, 0)

    def group(m, carry):
        wait_all(m, arrived, arrived_sem)
        loose_x = arrived[m].astype(F32).reshape(256, width)
        for h in range(width // 128):
            loose[h] = loose_x[:, 128 * h : 128 * (h + 1)]
        x = jnp.concatenate(
            [
                jnp.concatenate([loose[h, pl.ds(g, 64, stride=4), :] for h in range(width // 128)], axis=1)
                for g in range(4)
            ],
            axis=0,
        )
        x = attend(x, gain2[...], w_qk2[...], w_vt2[...], w_out2[...], bias2[...])
        x = feed(x, ffgain2[...], up2, down2)
        for g in range(4):
            for h in range(width // 128):
                loose[h, pl.ds(g, 64, stride=4), :] = x[64 * g : 64 * (g + 1), 128 * h : 128 * (h + 1)]
        y = jnp.concatenate([loose[h] for h in range(width // 128)], axis=1)
        returned[m] = y.reshape(peers, 16, width).astype(BF)
        send(m, returned, back, returned_sem, back_sem)
        return carry

    lax.fori_loop(0, chunks, group, 0)

    def finish(n, carry):
        cols_of = [[], [], [], []]
        for d in range(2):
            m = 2 * n + d
            wait_all(m, back, back_sem)
            y = back[m].astype(F32).reshape(WIN, 2, 2, WIN, width)
            for pp in range(2):
                halves = exchange(
                    y[:, 0, pp].reshape(WIN * WIN, width), y[:, 1, pp].reshape(WIN * WIN, width)
                )
                for e in range(2):
                    cols_of[2 * pp + e].append(halves[e].reshape(WIN, WIN, width))
        for p in range(4):
            at = pl.multiple_of(p * (cols // 4) + n * 2 * WIN, 2 * WIN)
            out[:, pl.ds(at, 2 * WIN), :] = jnp.concatenate(cols_of[p], axis=1).astype(BF)
        return carry

    lax.fori_loop(0, chunks // 2, finish, 0)

    def drain(m, carry):
        wait_all(m, sent, sent_sem)
        wait_all(m, returned, returned_sem)
        return carry

    lax.fori_loop(0, chunks, drain, 0)


def attention_operands(gain, w_qkv, w_out, bias):
    width = w_qkv.shape[0]
    return (
        gain[None],
        w_qkv[:, : 2 * width],
        w_qkv[:, 2 * width :].T,
        w_out,
        bias,
    )


def local(
    weather, pre_scale, pre_shift, w_expand, ex_scale, ex_shift, dw_kernel, dw_scale, dw_shift,
    w_project, win_gain, win_qkv, win_out, win_table, winff_gain, winff_up, winff_down,
    grid_gain, grid_qkv, grid_out, grid_table, gridff_gain, gridff_up, gridff_down,
):
    tile_rows, tile_cols, width = weather.shape
    wide = w_expand.shape[1]
    side = WIN
    rows_count = lax.axis_size("rows")
    cols_count = lax.axis_size("cols")
    ext = extended(weather, (("rows", 0), ("cols", 1)), 1)
    ext = jnp.pad(ext, ((0, 0), (PAD - 1, PAD - 1), (0, 0)))
    ri, ci = lax.axis_index("rows"), lax.axis_index("cols")
    valid = jnp.stack([ri > 0, ri < rows_count - 1, ci > 0, ci < cols_count - 1]).astype(F32)
    vmem = pl.BlockSpec(memory_space=pltpu.VMEM)
    biases = biases_keys_first(jnp.stack([win_table, grid_table]))
    chunks = tile_cols // 32
    slots = pltpu.VMEM((chunks, side * cols_count, 16, width), BF)
    return pl.pallas_call(
        functools.partial(block_kernel, quarter=rows_count // side),
        out_shape=jax.ShapeDtypeStruct((tile_rows, tile_cols, width), BF),
        in_specs=[pl.BlockSpec(memory_space=pltpu.SMEM)] + [vmem] * 26,
        out_specs=vmem,
        scratch_shapes=[
            pltpu.VMEM((tile_rows + 2, tile_cols + 2 * PAD, wide), BF),
            pltpu.VMEM((tile_cols, wide), BF),
            pltpu.VMEM((tile_rows, tile_cols, width), F32),
            slots,
            slots,
            slots,
            slots,
            pltpu.VMEM((width // 128, 256, 128), F32),
        ]
        + [pltpu.SemaphoreType.DMA((chunks,))] * 4,
        compiler_params=pltpu.CompilerParams(
            vmem_limit_bytes=50 << 20, collective_id=0, has_side_effects=True
        ),
        name="maxvit",
    )(
        valid, ext, pre_scale[None], pre_shift[None], w_expand, ex_scale[None], ex_shift[None],
        dw_kernel.reshape(9, wide), dw_scale[None], dw_shift[None], w_project,
        *attention_operands(win_gain, win_qkv, win_out, biases[0]),
        winff_gain[None], winff_up, winff_down,
        *attention_operands(grid_gain, grid_qkv, grid_out, biases[1]),
        gridff_gain[None], gridff_up, gridff_down,
    )


def solution(mesh):
    spread = P(("groups", "rows"), "cols", None)
    return jax.shard_map(
        local,
        mesh=mesh,
        in_specs=(spread,) + (P(),) * 23,
        out_specs=spread,
        check_vma=False,
    )
```

```python
import functools
import math

import jax
import jax.numpy as jnp
from jax import lax
from jax.experimental import pallas as pl
from jax.experimental.pallas import tpu as pltpu
from jax.sharding import PartitionSpec as P

WIN = 8
BF = jnp.bfloat16
F32 = jnp.float32
LOG2E = math.log2(math.e)
NT = (((1,), (1,)), ((), ()))
TN = (((0,), (0,)), ((), ()))


def biases_keys_first(tables):
    count, heads, offsets = tables.shape
    cells = WIN * WIN
    pair = jnp.arange(cells * cells)
    k, q = pair // cells, pair % cells
    offset = (q // WIN - k // WIN + WIN - 1) * (2 * WIN - 1) + (q % WIN - k % WIN + WIN - 1)
    onehot = (jnp.arange(offsets)[:, None] == offset[None, :]).astype(F32)
    flat = jnp.dot(
        tables.reshape(count * heads, offsets) * LOG2E, onehot, precision=lax.Precision.HIGHEST
    )
    flat = flat.reshape(count, heads, cells, cells).transpose(0, 2, 1, 3)
    return flat.reshape(count, cells, heads * cells)


def gelu(x):
    c0 = math.sqrt(2.0 / math.pi)
    inner = x * (c0 + (c0 * 0.044715) * (x * x))
    half = 0.5 * x
    return half + half * jnp.tanh(inner)


def norm(x, gain):
    center = x - jnp.mean(x, axis=-1, keepdims=True)
    spread = jnp.mean(center * center, axis=-1, keepdims=True)
    return (center * lax.rsqrt(spread + 1e-05) * gain).astype(BF)


def dot(a, b):
    return jnp.dot(a, b, preferred_element_type=F32)


def attend(x, gain, w_qk, w_vt, w_out, bias):
    width = x.shape[1]
    cells = WIN * WIN
    groups = x.shape[0] // cells
    heads = bias.shape[1] // cells
    dim = width // heads
    scale = dim ** (-0.5) * LOG2E
    n = norm(x, gain)
    qk = dot(n, w_qk).astype(BF)
    vt = lax.dot_general(w_vt, n, NT, preferred_element_type=F32).astype(BF)
    lane_head = lax.broadcasted_iota(jnp.int32, (cells, width), 1) // dim
    probs = []
    for g in range(groups):
        q = qk[g * cells : (g + 1) * cells, :width]
        k = qk[g * cells : (g + 1) * cells, width:]
        spread = jnp.concatenate(
            [jnp.where(lane_head == h, q, jnp.zeros_like(q)) for h in range(heads)], axis=0
        )
        s = lax.dot_general(k, spread, NT, preferred_element_type=F32) * scale + bias
        e = jnp.exp2(s - jnp.max(s, axis=0, keepdims=True))
        e = e * (1.0 / jnp.sum(e, axis=0, keepdims=True))
        probs.append(e.astype(BF))
    low = lax.broadcasted_iota(jnp.int32, (dim, 2 * cells), 1) < cells
    zeros = jnp.zeros((cells, 2 * cells), BF)
    mixed = []
    for g in range(0, groups, 2):
        parts = []
        for t in range(heads // 2):
            at = slice(2 * cells * t, 2 * cells * (t + 1))
            pair = jnp.concatenate(
                [
                    jnp.concatenate([probs[g][:, at], zeros], axis=1),
                    jnp.concatenate([zeros, probs[g + 1][:, at]], axis=1),
                ],
                axis=0,
            )
            v = vt[2 * dim * t : 2 * dim * (t + 1), g * cells : (g + 2) * cells]
            o = dot(v, pair)
            a, b = o[:, : 2 * cells], o[:, 2 * cells :]
            parts.append(jnp.where(low, a[:dim], pltpu.roll(b[:dim], cells, 1)))
            parts.append(jnp.where(low, pltpu.roll(a[dim:], cells, 1), b[dim:]))
        mixed.append(jnp.concatenate(parts, axis=0).astype(BF))
    mixed = jnp.concatenate(mixed, axis=1)
    return x + lax.dot_general(mixed, w_out, TN, preferred_element_type=F32)


def feed(x, gain, up_ref, down_ref, step=256):
    n = norm(x, gain)
    total = x
    for at in range(0, up_ref.shape[1], step):
        hidden = gelu(dot(n, up_ref[:, at : at + step])).astype(BF)
        total = total + dot(hidden, down_ref[at : at + step, :])
    return total


PAD = 16


def block_kernel(
    weather, pre_scale, pre_shift, w_expand, ex_scale, ex_shift, taps, dw_scale, dw_shift,
    w_project, gain, w_qk, w_vt, w_out, bias, ffgain, up, down, gain2, w_qk2, w_vt2, w_out2,
    bias2, ffgain2, up2, down2, out, grown, depth, one, sent, arrived, returned, back, loose,
    halo_rows, halo_cols, halo_send, halo_recv, sent_sem, arrived_sem, returned_sem, back_sem, *, quarter,
):
    row_at, col_at = lax.axis_index("rows"), lax.axis_index("cols")
    col_count = lax.axis_size("cols")
    peers = WIN * col_count
    me = (row_at // quarter) * col_count + col_at

    def place(peer):
        return {
            "rows": (peer // col_count) * quarter + lax.rem(row_at, quarter),
            "cols": lax.rem(peer, col_count),
        }

    barrier = pltpu.get_barrier_semaphore()

    def greet(k, carry):
        pl.semaphore_signal(
            barrier, 1, device_id=place(lax.rem(me + k, peers)),
            device_id_type=pl.DeviceIdType.MESH,
        )
        return carry

    lax.fori_loop(1, peers, greet, 0)
    rows, cols, width = out.shape
    row_count = lax.axis_size("rows")

    def exists(dr, dc):
        r, c = row_at + dr, col_at + dc
        return (r >= 0) & (r < row_count) & (c >= 0) & (c < col_count)

    around = [(dr, dc) for dr in (-1, 0, 1) for dc in (-1, 0, 1) if (dr, dc) != (0, 0)]

    def edge_copy(k):
        dr, dc = around[k]
        row = {-1: 0, 0: slice(None), 1: rows - 1}[dr]
        if dc == 0:
            src, dst = weather.at[row], halo_rows.at[0 if dr > 0 else 1]
        else:
            side = 0 if dc > 0 else 1
            src = weather.at[row, pl.ds(cols - PAD if dc > 0 else 0, PAD)]
            dst = halo_cols.at[side, {-1: rows + 1, 0: pl.ds(1, rows), 1: 0}[dr]]
        return pltpu.make_async_remote_copy(
            src_ref=src, dst_ref=dst, send_sem=halo_send.at[k], recv_sem=halo_recv.at[k],
            device_id={"rows": row_at + dr, "cols": col_at + dc},
            device_id_type=pl.DeviceIdType.MESH,
        )

    greeted = peers - 1
    for dr, dc in around:
        if dr != 0 and quarter > 1:
            greeted = greeted + exists(dr, dc).astype(jnp.int32)

            @pl.when(exists(dr, dc))
            def _():
                pl.semaphore_signal(
                    barrier, 1, device_id={"rows": row_at + dr, "cols": col_at + dc},
                    device_id_type=pl.DeviceIdType.MESH,
                )

    pl.semaphore_wait(barrier, greeted)
    for k, (dr, dc) in enumerate(around):

        @pl.when(exists(dr, dc))
        def _():
            edge_copy(k).start()


    def send(m, src, dst, src_sem, dst_sem):
        def one_peer(k, carry):
            peer = lax.rem(me + k, peers)
            pltpu.make_async_remote_copy(
                src_ref=src.at[m, peer],
                dst_ref=dst.at[m, me],
                send_sem=src_sem.at[m],
                recv_sem=dst_sem.at[m],
                device_id=place(peer),
                device_id_type=pl.DeviceIdType.MESH,
            ).start()
            return carry

        lax.fori_loop(1, peers, one_peer, 0)
        dst[m, me] = src[m, me]

    def wait_all(m, ref, sem):
        part = ref.at[m, pl.ds(0, peers - 1)]
        pltpu.make_async_copy(part, part, sem.at[m]).wait()

    wide = w_expand.shape[1]

    def grow(x, store):
        x = (x.astype(F32) * pre_scale[...] + pre_shift[...]).astype(BF)
        for at in range(0, wide, 256):
            s = slice(at, at + 256)
            store(s, gelu(dot(x, w_expand[:, s]) * ex_scale[:, s] + ex_shift[:, s]))

    def expand(r, carry):
        def store(s, y):
            grown[r + 1, PAD : PAD + cols, s] = y.astype(BF)

        grow(weather[r], store)
        return carry

    lax.fori_loop(0, rows, expand, 0)
    for k, (dr, dc) in enumerate(around):

        @pl.when(exists(-dr, -dc))
        def _():
            edge_copy(k).wait_recv()

    def expand_row(d, carry):
        keep = jnp.where(d == 0, row_at, row_count - 1 - row_at) > 0

        def store(s, y):
            grown[d * (rows + 1), PAD : PAD + cols, s] = jnp.where(keep, y, 0.0).astype(BF)

        grow(halo_rows[d], store)
        return carry

    lax.fori_loop(0, 2, expand_row, 0)
    line = lax.broadcasted_iota(jnp.int32, ((rows + 2) * PAD, 256), 0) // PAD
    inside = ((line > 0) | (row_at > 0)) & ((line < rows + 1) | (row_at < row_count - 1))
    for side in range(2):
        keep = inside & ((col_at > 0) if side == 0 else (col_at < col_count - 1))

        def store(s, y):
            y = jnp.where(keep, y, 0.0).astype(BF).reshape(rows + 2, PAD, 256)
            grown[:, (PAD + cols) * side : (PAD + cols) * side + PAD, s] = y

        grow(halo_cols[side].reshape((rows + 2) * PAD, width), store)

    strip = cols // 8

    def row(step, carry):
        part, r = step // rows, lax.rem(step, rows)
        for g in range(4):
            c = pl.multiple_of(g * 2 * strip + part * strip, 16)
            for lane in range(0, wide, 128):
                ls = slice(lane, lane + 128)
                sums = [None] * 3
                for a in range(3):
                    e = grown[r + a, pl.ds(c, strip + 2 * PAD), ls].astype(F32)
                    e = e[PAD - 8 : PAD + strip + 8]
                    for b in range(3):
                        term = e * taps[3 * a + b : 3 * a + b + 1, ls]
                        sums[b] = term if a == 0 else sums[b] + term
                total = sums[0][7 : 7 + strip] + sums[1][8 : 8 + strip] + sums[2][9 : 9 + strip]
                depth[strip * g : strip * (g + 1), ls] = gelu(
                    total * dw_scale[:, ls] + dw_shift[:, ls]
                ).astype(BF)
        y = dot(depth[...], w_project[...])
        for g in range(4):
            c = pl.multiple_of(g * 2 * strip + part * strip, 16)
            z = weather[r, pl.ds(c, strip), :].astype(F32) + y[strip * g : strip * (g + 1)]
            one[r, pl.ds(c, strip), :] = z.astype(BF).astype(F32)
        return carry

    first_half = lax.rem(lax.broadcasted_iota(jnp.int32, (WIN * WIN, width), 0), WIN) < WIN // 2
    half = WIN // 2
    chunks = cols // 32

    def exchange(a, b):
        firsts = jnp.where(first_half, a, pltpu.roll(b, half, 0))
        seconds = jnp.where(first_half, pltpu.roll(a, WIN * WIN - half, 0), b)
        return firsts, seconds

    def window(m, carry):
        pieces = []
        for g in range(4):
            at = pl.multiple_of(g * (cols // 4) + m * WIN, WIN)
            pieces.append(one[:, pl.ds(at, WIN), :].reshape(WIN * WIN, width))
        x = jnp.concatenate(pieces, axis=0)
        x = attend(x, gain[...], w_qk[...], w_vt[...], w_out[...], bias[...])
        x = feed(x, ffgain[...], up, down)
        x = [x[WIN * WIN * g : WIN * WIN * (g + 1)] for g in range(4)]
        low, high = exchange(x[0], x[1]), exchange(x[2], x[3])
        for c in range(2):
            y = jnp.concatenate(
                [low[c].reshape(WIN, WIN, width), high[c].reshape(WIN, WIN, width)], axis=1
            ).astype(BF)
            for i in range(WIN):
                sent[m, i * 2 + c] = y[i]
        send(m, sent, arrived, sent_sem, arrived_sem)
        return carry

    def part(p, carry):
        lax.fori_loop(p * rows, (p + 1) * rows, row, 0)
        lax.fori_loop(p * (chunks // 2), (p + 1) * (chunks // 2), window, 0)
        return carry

    lax.fori_loop(0, 2, part, 0)

    def group(m, carry):
        wait_all(m, arrived, arrived_sem)
        loose_x = arrived[m].astype(F32).reshape(256, width)
        for h in range(width // 128):
            loose[h] = loose_x[:, 128 * h : 128 * (h + 1)]
        x = jnp.concatenate(
            [
                jnp.concatenate([loose[h, pl.ds(g, 64, stride=4), :] for h in range(width // 128)], axis=1)
                for g in range(4)
            ],
            axis=0,
        )
        x = attend(x, gain2[...], w_qk2[...], w_vt2[...], w_out2[...], bias2[...])
        x = feed(x, ffgain2[...], up2, down2)
        for g in range(4):
            for h in range(width // 128):
                loose[h, pl.ds(g, 64, stride=4), :] = x[64 * g : 64 * (g + 1), 128 * h : 128 * (h + 1)]
        y = jnp.concatenate([loose[h] for h in range(width // 128)], axis=1)
        returned[m] = y.reshape(peers, 16, width).astype(BF)
        send(m, returned, back, returned_sem, back_sem)
        return carry

    lax.fori_loop(0, chunks, group, 0)

    def finish(n, carry):
        cols_of = [[], [], [], []]
        for d in range(2):
            m = 2 * n + d
            wait_all(m, back, back_sem)
            y = back[m].astype(F32).reshape(WIN, 2, 2, WIN, width)
            for pp in range(2):
                halves = exchange(
                    y[:, 0, pp].reshape(WIN * WIN, width), y[:, 1, pp].reshape(WIN * WIN, width)
                )
                for e in range(2):
                    cols_of[2 * pp + e].append(halves[e].reshape(WIN, WIN, width))
        for p in range(4):
            at = pl.multiple_of(p * (cols // 4) + n * 2 * WIN, 2 * WIN)
            out[:, pl.ds(at, 2 * WIN), :] = jnp.concatenate(cols_of[p], axis=1).astype(BF)
        return carry

    lax.fori_loop(0, chunks // 2, finish, 0)

    def drain(m, carry):
        wait_all(m, sent, sent_sem)
        wait_all(m, returned, returned_sem)
        return carry

    lax.fori_loop(0, chunks, drain, 0)
    for k, (dr, dc) in enumerate(around):

        @pl.when(exists(dr, dc))
        def _():
            edge_copy(k).wait_send()


def attention_operands(gain, w_qkv, w_out, bias):
    width = w_qkv.shape[0]
    return (
        gain[None],
        w_qkv[:, : 2 * width],
        w_qkv[:, 2 * width :].T,
        w_out,
        bias,
    )


def local(
    weather, pre_scale, pre_shift, w_expand, ex_scale, ex_shift, dw_kernel, dw_scale, dw_shift,
    w_project, win_gain, win_qkv, win_out, win_table, winff_gain, winff_up, winff_down,
    grid_gain, grid_qkv, grid_out, grid_table, gridff_gain, gridff_up, gridff_down,
):
    tile_rows, tile_cols, width = weather.shape
    wide = w_expand.shape[1]
    side = WIN
    rows_count = lax.axis_size("rows")
    cols_count = lax.axis_size("cols")
    vmem = pl.BlockSpec(memory_space=pltpu.VMEM)
    biases = biases_keys_first(jnp.stack([win_table, grid_table]))
    chunks = tile_cols // 32
    slots = pltpu.VMEM((chunks, side * cols_count, 16, width), BF)
    return pl.pallas_call(
        functools.partial(block_kernel, quarter=rows_count // side),
        out_shape=jax.ShapeDtypeStruct((tile_rows, tile_cols, width), BF),
        in_specs=[vmem] * 26,
        out_specs=vmem,
        scratch_shapes=[
            pltpu.VMEM((tile_rows + 2, tile_cols + 2 * PAD, wide), BF),
            pltpu.VMEM((tile_cols // 2, wide), BF),
            pltpu.VMEM((tile_rows, tile_cols, width), F32),
            slots,
            slots,
            slots,
            slots,
            pltpu.VMEM((width // 128, 256, 128), F32),
            pltpu.VMEM((2, tile_cols, width), BF),
            pltpu.VMEM((2, tile_rows + 2, PAD, width), BF),
            pltpu.SemaphoreType.DMA((8,)),
            pltpu.SemaphoreType.DMA((8,)),
        ]
        + [pltpu.SemaphoreType.DMA((chunks,))] * 4,
        compiler_params=pltpu.CompilerParams(
            vmem_limit_bytes=50 << 20, collective_id=0, has_side_effects=True
        ),
        name="maxvit",
    )(
        weather, pre_scale[None], pre_shift[None], w_expand, ex_scale[None], ex_shift[None],
        dw_kernel.reshape(9, wide), dw_scale[None], dw_shift[None], w_project,
        *attention_operands(win_gain, win_qkv, win_out, biases[0]),
        winff_gain[None], winff_up, winff_down,
        *attention_operands(grid_gain, grid_qkv, grid_out, biases[1]),
        gridff_gain[None], gridff_up, gridff_down,
    )


def solution(mesh):
    spread = P(("groups", "rows"), "cols", None)
    return jax.shard_map(
        local,
        mesh=mesh,
        in_specs=(spread,) + (P(),) * 23,
        out_specs=spread,
        check_vma=False,
    )
```

```python
import functools
import math

import jax
import jax.numpy as jnp
from jax import lax
from jax.experimental import pallas as pl
from jax.experimental.pallas import tpu as pltpu
from jax.sharding import PartitionSpec as P

WIN = 8
BF = jnp.bfloat16
F32 = jnp.float32
LOG2E = math.log2(math.e)
NT = (((1,), (1,)), ((), ()))
TN = (((0,), (0,)), ((), ()))


def biases_keys_first(tables):
    count, heads, offsets = tables.shape
    cells = WIN * WIN
    pair = jnp.arange(cells * cells)
    k, q = pair // cells, pair % cells
    offset = (q // WIN - k // WIN + WIN - 1) * (2 * WIN - 1) + (q % WIN - k % WIN + WIN - 1)
    onehot = (jnp.arange(offsets)[:, None] == offset[None, :]).astype(F32)
    flat = jnp.dot(
        tables.reshape(count * heads, offsets) * LOG2E, onehot, precision=lax.Precision.HIGHEST
    )
    flat = flat.reshape(count, heads, cells, cells).transpose(0, 2, 1, 3)
    return flat.reshape(count, cells, heads * cells)


def gelu(x):
    c0 = math.sqrt(2.0 / math.pi)
    inner = x * (c0 + (c0 * 0.044715) * (x * x))
    half = 0.5 * x
    return half + half * jnp.tanh(inner)


def norm(x, gain):
    center = x - jnp.mean(x, axis=-1, keepdims=True)
    spread = jnp.mean(center * center, axis=-1, keepdims=True)
    return (center * lax.rsqrt(spread + 1e-05) * gain).astype(BF)


def dot(a, b):
    return jnp.dot(a, b, preferred_element_type=F32)


def attend(x, gain, w_qk, w_vt, w_out, bias):
    width = x.shape[1]
    cells = WIN * WIN
    groups = x.shape[0] // cells
    heads = bias.shape[1] // cells
    dim = width // heads
    scale = dim ** (-0.5) * LOG2E
    n = norm(x, gain)
    qk = dot(n, w_qk).astype(BF)
    vt = lax.dot_general(w_vt, n, NT, preferred_element_type=F32).astype(BF)
    lane_head = lax.broadcasted_iota(jnp.int32, (cells, width), 1) // dim
    probs = []
    for g in range(groups):
        q = qk[g * cells : (g + 1) * cells, :width]
        k = qk[g * cells : (g + 1) * cells, width:]
        spread = jnp.concatenate(
            [jnp.where(lane_head == h, q, jnp.zeros_like(q)) for h in range(heads)], axis=0
        )
        s = lax.dot_general(k, spread, NT, preferred_element_type=F32) * scale + bias
        e = jnp.exp2(s - jnp.max(s, axis=0, keepdims=True))
        e = e * (1.0 / jnp.sum(e, axis=0, keepdims=True))
        probs.append(e.astype(BF))
    low = lax.broadcasted_iota(jnp.int32, (dim, 2 * cells), 1) < cells
    zeros = jnp.zeros((cells, 2 * cells), BF)
    mixed = []
    for g in range(0, groups, 2):
        parts = []
        for t in range(heads // 2):
            at = slice(2 * cells * t, 2 * cells * (t + 1))
            pair = jnp.concatenate(
                [
                    jnp.concatenate([probs[g][:, at], zeros], axis=1),
                    jnp.concatenate([zeros, probs[g + 1][:, at]], axis=1),
                ],
                axis=0,
            )
            v = vt[2 * dim * t : 2 * dim * (t + 1), g * cells : (g + 2) * cells]
            o = dot(v, pair)
            a, b = o[:, : 2 * cells], o[:, 2 * cells :]
            parts.append(jnp.where(low, a[:dim], pltpu.roll(b[:dim], cells, 1)))
            parts.append(jnp.where(low, pltpu.roll(a[dim:], cells, 1), b[dim:]))
        mixed.append(jnp.concatenate(parts, axis=0).astype(BF))
    mixed = jnp.concatenate(mixed, axis=1)
    return x + lax.dot_general(mixed, w_out, TN, preferred_element_type=F32)


def feed(x, gain, up_ref, down_ref, step=256):
    n = norm(x, gain)
    total = x
    for at in range(0, up_ref.shape[1], step):
        hidden = gelu(dot(n, up_ref[:, at : at + step])).astype(BF)
        total = total + dot(hidden, down_ref[at : at + step, :])
    return total


PAD = 16


def block_kernel(
    weather, pre_scale, pre_shift, w_expand, ex_scale, ex_shift, taps, dw_scale, dw_shift,
    w_project, gain, w_qk, w_vt, w_out, bias, ffgain, up, down, gain2, w_qk2, w_vt2, w_out2,
    bias2, ffgain2, up2, down2, out, grown, depth, one, sent, arrived, returned, back, loose,
    halo_rows, halo_cols, halo_send, halo_recv, sent_sem, arrived_sem, returned_sem, back_sem, *, quarter,
):
    row_at, col_at = lax.axis_index("rows"), lax.axis_index("cols")
    col_count = lax.axis_size("cols")
    peers = WIN * col_count
    me = (row_at // quarter) * col_count + col_at

    def place(peer):
        return {
            "rows": (peer // col_count) * quarter + lax.rem(row_at, quarter),
            "cols": lax.rem(peer, col_count),
        }

    barrier = pltpu.get_barrier_semaphore()

    def greet(k, carry):
        pl.semaphore_signal(
            barrier, 1, device_id=place(lax.rem(me + k, peers)),
            device_id_type=pl.DeviceIdType.MESH,
        )
        return carry

    lax.fori_loop(1, peers, greet, 0)
    rows, cols, width = out.shape
    row_count = lax.axis_size("rows")

    def exists(dr, dc):
        r, c = row_at + dr, col_at + dc
        return (r >= 0) & (r < row_count) & (c >= 0) & (c < col_count)

    around = [(dr, dc) for dr in (-1, 0, 1) for dc in (-1, 0, 1) if (dr, dc) != (0, 0)]

    def edge_copy(k):
        dr, dc = around[k]
        row = {-1: 0, 0: slice(None), 1: rows - 1}[dr]
        if dc == 0:
            src, dst = weather.at[row], halo_rows.at[0 if dr > 0 else 1]
        else:
            side = 0 if dc > 0 else 1
            src = weather.at[row, pl.ds(cols - PAD if dc > 0 else 0, PAD)]
            dst = halo_cols.at[side, {-1: rows + 1, 0: pl.ds(1, rows), 1: 0}[dr]]
        return pltpu.make_async_remote_copy(
            src_ref=src, dst_ref=dst, send_sem=halo_send.at[k], recv_sem=halo_recv.at[k],
            device_id={"rows": row_at + dr, "cols": col_at + dc},
            device_id_type=pl.DeviceIdType.MESH,
        )

    greeted = peers - 1
    for dr, dc in around:
        if dr != 0 and quarter > 1:
            greeted = greeted + exists(dr, dc).astype(jnp.int32)

            @pl.when(exists(dr, dc))
            def _():
                pl.semaphore_signal(
                    barrier, 1, device_id={"rows": row_at + dr, "cols": col_at + dc},
                    device_id_type=pl.DeviceIdType.MESH,
                )

    pl.semaphore_wait(barrier, greeted)
    for k, (dr, dc) in enumerate(around):

        @pl.when(exists(dr, dc))
        def _():
            edge_copy(k).start()


    def send(m, src, dst, src_sem, dst_sem):
        def one_peer(k, carry):
            peer = lax.rem(me + k, peers)
            pltpu.make_async_remote_copy(
                src_ref=src.at[m, peer],
                dst_ref=dst.at[m, me],
                send_sem=src_sem.at[m],
                recv_sem=dst_sem.at[m],
                device_id=place(peer),
                device_id_type=pl.DeviceIdType.MESH,
            ).start()
            return carry

        lax.fori_loop(1, peers, one_peer, 0)
        dst[m, me] = src[m, me]

    def wait_all(m, ref, sem):
        part = ref.at[m, pl.ds(0, peers - 1)]
        pltpu.make_async_copy(part, part, sem.at[m]).wait()

    wide = w_expand.shape[1]

    def grow(x, store):
        x = (x.astype(F32) * pre_scale[...] + pre_shift[...]).astype(BF)
        for at in range(0, wide, 256):
            s = slice(at, at + 256)
            store(s, gelu(dot(x, w_expand[:, s]) * ex_scale[:, s] + ex_shift[:, s]))

    def expand(r, carry):
        def store(s, y):
            grown[r + 1, PAD : PAD + cols, s] = y.astype(BF)

        grow(weather[r], store)
        return carry

    lax.fori_loop(0, rows, expand, 0)
    for k, (dr, dc) in enumerate(around):

        @pl.when(exists(-dr, -dc))
        def _():
            edge_copy(k).wait_recv()

    def expand_row(d, carry):
        keep = jnp.where(d == 0, row_at, row_count - 1 - row_at) > 0

        def store(s, y):
            grown[d * (rows + 1), PAD : PAD + cols, s] = jnp.where(keep, y, 0.0).astype(BF)

        grow(halo_rows[d], store)
        return carry

    lax.fori_loop(0, 2, expand_row, 0)
    line = lax.broadcasted_iota(jnp.int32, ((rows + 2) * PAD, 256), 0) // PAD
    inside = ((line > 0) | (row_at > 0)) & ((line < rows + 1) | (row_at < row_count - 1))
    for side in range(2):
        keep = inside & ((col_at > 0) if side == 0 else (col_at < col_count - 1))

        def store(s, y):
            y = jnp.where(keep, y, 0.0).astype(BF).reshape(rows + 2, PAD, 256)
            grown[:, (PAD + cols) * side : (PAD + cols) * side + PAD, s] = y

        grow(halo_cols[side].reshape((rows + 2) * PAD, width), store)

    strip = cols // 8

    def row(step, carry):
        part, r = step // rows, lax.rem(step, rows)
        for g in range(4):
            c = pl.multiple_of(g * 2 * strip + part * strip, 16)
            for lane in range(0, wide, 128):
                ls = slice(lane, lane + 128)
                sums = [None] * 3
                for a in range(3):
                    e = grown[r + a, pl.ds(c, strip + 2 * PAD), ls].astype(F32)
                    e = e[PAD - 8 : PAD + strip + 8]
                    for b in range(3):
                        term = e * taps[a, b : b + 1, ls]
                        sums[b] = term if a == 0 else sums[b] + term
                total = sums[0][7 : 7 + strip] + sums[1][8 : 8 + strip] + sums[2][9 : 9 + strip]
                depth[strip * g : strip * (g + 1), ls] = gelu(
                    total * dw_scale[:, ls] + dw_shift[:, ls]
                ).astype(BF)
        y = dot(depth[...], w_project[...])
        for g in range(4):
            c = pl.multiple_of(g * 2 * strip + part * strip, 16)
            z = weather[r, pl.ds(c, strip), :].astype(F32) + y[strip * g : strip * (g + 1)]
            one[r, pl.ds(c, strip), :] = z.astype(BF).astype(F32)
        return carry

    first_half = lax.rem(lax.broadcasted_iota(jnp.int32, (WIN * WIN, width), 0), WIN) < WIN // 2
    half = WIN // 2
    chunks = cols // 32

    def exchange(a, b):
        firsts = jnp.where(first_half, a, pltpu.roll(b, half, 0))
        seconds = jnp.where(first_half, pltpu.roll(a, WIN * WIN - half, 0), b)
        return firsts, seconds

    def window(m, carry):
        pieces = []
        for g in range(4):
            at = pl.multiple_of(g * (cols // 4) + m * WIN, WIN)
            pieces.append(one[:, pl.ds(at, WIN), :].reshape(WIN * WIN, width))
        x = jnp.concatenate(pieces, axis=0)
        x = attend(x, gain[...], w_qk[:, : 2 * width], w_vt[...], w_out[...], bias[0])
        x = feed(x, ffgain[...], up, down)
        x = [x[WIN * WIN * g : WIN * WIN * (g + 1)] for g in range(4)]
        low, high = exchange(x[0], x[1]), exchange(x[2], x[3])
        for c in range(2):
            y = jnp.concatenate(
                [low[c].reshape(WIN, WIN, width), high[c].reshape(WIN, WIN, width)], axis=1
            ).astype(BF)
            for i in range(WIN):
                sent[m, i * 2 + c] = y[i]
        send(m, sent, arrived, sent_sem, arrived_sem)
        return carry

    def part(p, carry):
        lax.fori_loop(p * rows, (p + 1) * rows, row, 0)
        lax.fori_loop(p * (chunks // 2), (p + 1) * (chunks // 2), window, 0)
        return carry

    lax.fori_loop(0, 2, part, 0)

    def group(m, carry):
        wait_all(m, arrived, arrived_sem)
        loose_x = arrived[m].astype(F32).reshape(256, width)
        for h in range(width // 128):
            loose[h] = loose_x[:, 128 * h : 128 * (h + 1)]
        x = jnp.concatenate(
            [
                jnp.concatenate([loose[h, pl.ds(g, 64, stride=4), :] for h in range(width // 128)], axis=1)
                for g in range(4)
            ],
            axis=0,
        )
        x = attend(x, gain2[...], w_qk2[:, : 2 * width], w_vt2[...], w_out2[...], bias2[1])
        x = feed(x, ffgain2[...], up2, down2)
        for g in range(4):
            for h in range(width // 128):
                loose[h, pl.ds(g, 64, stride=4), :] = x[64 * g : 64 * (g + 1), 128 * h : 128 * (h + 1)]
        y = jnp.concatenate([loose[h] for h in range(width // 128)], axis=1)
        returned[m] = y.reshape(peers, 16, width).astype(BF)
        send(m, returned, back, returned_sem, back_sem)
        return carry

    lax.fori_loop(0, chunks, group, 0)

    def finish(n, carry):
        cols_of = [[], [], [], []]
        for d in range(2):
            m = 2 * n + d
            wait_all(m, back, back_sem)
            y = back[m].astype(F32).reshape(WIN, 2, 2, WIN, width)
            for pp in range(2):
                halves = exchange(
                    y[:, 0, pp].reshape(WIN * WIN, width), y[:, 1, pp].reshape(WIN * WIN, width)
                )
                for e in range(2):
                    cols_of[2 * pp + e].append(halves[e].reshape(WIN, WIN, width))
        for p in range(4):
            at = pl.multiple_of(p * (cols // 4) + n * 2 * WIN, 2 * WIN)
            out[:, pl.ds(at, 2 * WIN), :] = jnp.concatenate(cols_of[p], axis=1).astype(BF)
        return carry

    lax.fori_loop(0, chunks // 2, finish, 0)

    def drain(m, carry):
        wait_all(m, sent, sent_sem)
        wait_all(m, returned, returned_sem)
        return carry

    lax.fori_loop(0, chunks, drain, 0)
    for k, (dr, dc) in enumerate(around):

        @pl.when(exists(dr, dc))
        def _():
            edge_copy(k).wait_send()


def attention_operands(gain, w_qkv, w_out, bias):
    width = w_qkv.shape[0]
    return (
        gain[None],
        w_qkv,
        w_qkv[:, 2 * width :].T,
        w_out,
        bias,
    )


def local(
    weather, pre_scale, pre_shift, w_expand, ex_scale, ex_shift, dw_kernel, dw_scale, dw_shift,
    w_project, win_gain, win_qkv, win_out, win_table, winff_gain, winff_up, winff_down,
    grid_gain, grid_qkv, grid_out, grid_table, gridff_gain, gridff_up, gridff_down,
):
    tile_rows, tile_cols, width = weather.shape
    wide = w_expand.shape[1]
    side = WIN
    rows_count = lax.axis_size("rows")
    cols_count = lax.axis_size("cols")
    vmem = pl.BlockSpec(memory_space=pltpu.VMEM)
    biases = biases_keys_first(jnp.stack([win_table, grid_table]))
    chunks = tile_cols // 32
    slots = pltpu.VMEM((chunks, side * cols_count, 16, width), BF)
    return pl.pallas_call(
        functools.partial(block_kernel, quarter=rows_count // side),
        out_shape=jax.ShapeDtypeStruct((tile_rows, tile_cols, width), BF),
        in_specs=[vmem] * 26,
        out_specs=vmem,
        scratch_shapes=[
            pltpu.VMEM((tile_rows + 2, tile_cols + 2 * PAD, wide), BF),
            pltpu.VMEM((tile_cols // 2, wide), BF),
            pltpu.VMEM((tile_rows, tile_cols, width), F32),
            slots,
            slots,
            slots,
            slots,
            pltpu.VMEM((width // 128, 256, 128), F32),
            pltpu.VMEM((2, tile_cols, width), BF),
            pltpu.VMEM((2, tile_rows + 2, PAD, width), BF),
            pltpu.SemaphoreType.DMA((8,)),
            pltpu.SemaphoreType.DMA((8,)),
        ]
        + [pltpu.SemaphoreType.DMA((chunks,))] * 4,
        compiler_params=pltpu.CompilerParams(
            vmem_limit_bytes=50 << 20, collective_id=0, has_side_effects=True
        ),
        name="maxvit",
    )(
        weather, pre_scale[None], pre_shift[None], w_expand, ex_scale[None], ex_shift[None],
        dw_kernel, dw_scale[None], dw_shift[None], w_project,
        *attention_operands(win_gain, win_qkv, win_out, biases),
        winff_gain[None], winff_up, winff_down,
        *attention_operands(grid_gain, grid_qkv, grid_out, biases),
        gridff_gain[None], gridff_up, gridff_down,
    )


def solution(mesh):
    spread = P(("groups", "rows"), "cols", None)
    return jax.shard_map(
        local,
        mesh=mesh,
        in_specs=(spread,) + (P(),) * 23,
        out_specs=spread,
        check_vma=False,
    )
```
